512 devices in a mesh: ctx: 64 (over z, x), tp: 8 (over y, core).
Axes of the slice: x: 4, y: 4, z: 16, core: 2. Of those that a mesh axis runs over, the one named last changes fastest.
Arguments:
- tokens: bfloat16 [8192, 3072], P('ctx'), may hold values from -6 to 6
- w_qkv: bfloat16 [3072, 3, 3072], P('ctx', None, 'tp'), may hold values from -0.109375 to 0.109375
- w_rate: bfloat16 [3072, 48], P('ctx', 'tp'), may hold values from -0.109375 to 0.109375
- layer_one: float32 [48, 64, 256], P('tp'), may hold values from -0.75 to 0.75
- layer_two: float32 [48, 64, 256], P('tp'), may hold values from -0.375 to 0.375
- bias_one: float32 [48, 256], P('tp'), may hold values from -3 to 3
- bias_two: float32 [48, 64], P('tp'), may hold values from -3 to 3
- inner_gain: float32 [48, 64], P('tp'), may hold values from 0.3 to 3
- inner_bias: float32 [48, 64], P('tp'), may hold values from -3 to 3
- inner_rate: float32 [48], P('tp'), may hold values from 0.03 to 0.3
- out_gain: float32 [3072], P('tp'), may hold values from 0.25 to 1.75
Outputs:
- mixed: bfloat16 [8192, 3072], P('ctx', 'tp')
The draws below stay inside these ranges and needn't reach their ends.
All inputs are finite; a program needn't handle non-finite values.
Results may differ from the reference program's by a relative error of at most 0.0045.
Values may be sent and summed in bfloat16 or wider, within the bound.
No kernel may reach another device: no remote copies, remote signals or barrier semaphores. Data moves between devices by JAX's collectives and lax.ppermute only.
A program may use at most 64 MiB of HBM per device.

```python
import math
import jax
import jax.numpy as jnp
from jax import lax

D = 3072
HEADS = 48
HD = 64
HID = 256
TOK_DEV = 128
CHAIN = 8
MB = 32
CLIPS = 8
TOKENS = 8192


def shard_levels(key, extent, shards, smallest, top_value):
    def one(position, blocks):
        draws = jax.random.uniform(jax.random.fold_in(jax.random.fold_in(key, 6), position), (blocks,), jnp.float32, smallest / len(shards), top_value / len(shards))
        return jnp.repeat(jnp.exp(draws), extent[position] // blocks).reshape((-1,) + (1,) * (len(extent) - position - 1))

    level = one(*shards[0])
    for cut in shards[1:]:
        level = level * one(*cut)
    return level


def centred(own_key, extent, scale, most, cuts=(), kind=jnp.bfloat16):
    drawn = jax.random.normal(own_key, extent, jnp.float32) * scale
    if len(cuts) > 0:
        drawn = shard_levels(own_key, extent, cuts, -0.22, 0.18) * drawn
    return jnp.clip(drawn, min=-most, max=most).astype(kind)


def setup_inputs(seed: int = 0) -> dict:
    key_list = jax.random.split(jax.random.key(seed), 12)
    tokens = centred(key_list[0], (TOKENS, D), 1.0, 6.0, ((0, 64),))
    w_qkv = centred(key_list[1], (D, 3, HEADS * HD), D ** -0.5, 0.109375, ((0, 64), (2, 8)))
    w_rate = centred(key_list[2], (D, HEADS), D ** -0.5, 0.109375, ((0, 64), (1, 8)))
    layer_one = centred(key_list[3], (HEADS, HD, HID), HD ** -0.5, 0.75, ((0, 8),), jnp.float32)
    layer_two = centred(key_list[4], (HEADS, HD, HID), HID ** -0.5, 0.375, ((0, 8),), jnp.float32)
    bias_one = centred(key_list[5], (HEADS, HID), 0.5, 3.0, ((0, 8),), jnp.float32)
    bias_two = centred(key_list[6], (HEADS, HD), 0.5, 3.0, ((0, 8),), jnp.float32)
    inner_gain = jnp.clip(jnp.exp(math.log(3.0) - 2.3025851 * jax.random.uniform(key_list[7], (HEADS, HD), jnp.float32) ** shard_levels(key_list[7], (HEADS, HD), ((0, 8),), -0.2, 0.2)), 0.3, 3.0)
    inner_bias = centred(key_list[8], (HEADS, HD), 0.5, 3.0, ((0, 8),), jnp.float32)
    inner_rate = jnp.clip(jnp.exp(math.log(0.3) - 2.3025852 * jax.random.uniform(key_list[9], (HEADS,), jnp.float32) ** shard_levels(key_list[9], (HEADS,), ((0, 8),), -0.2, 0.2)), 0.03, 0.3)
    out_gain = jnp.clip(1.0 + 0.15 * jax.random.normal(key_list[10], (D,), jnp.float32), 0.25, 1.75)
    return {"tokens": tokens, "w_qkv": w_qkv, "w_rate": w_rate, "layer_one": layer_one, "layer_two": layer_two, "bias_one": bias_one, "bias_two": bias_two, "inner_gain": inner_gain, "inner_bias": inner_bias, "inner_rate": inner_rate, "out_gain": out_gain}


def head_forward(inner_state, inputs, gain_row, bias_row):
    first_w, second_w, first_b, second_b = inner_state
    hidden = jnp.dot(inputs, first_w, precision=lax.Precision.HIGHEST) + first_b
    active = jax.nn.gelu(hidden, approximate=True)
    mapped = lax.dot_general(active, second_w, (((1,), (1,)), ((), ())), precision=lax.Precision.HIGHEST) + second_b
    centre = mapped - lax.optimization_barrier(jnp.mean(mapped, -1, keepdims=True))
    spread = lax.optimization_barrier(jnp.mean(centre * centre, -1, keepdims=True))
    return gain_row * centre * lax.rsqrt(spread + 1e-06) + bias_row

def inner_step(inner_state, mini_batch, gain_row, bias_row):
    key_rows, value_rows, query_rows, rate_rows = mini_batch
    target = value_rows - key_rows

    def recon_loss(params):
        residual = head_forward(params, key_rows, gain_row, bias_row) - target
        return 0.5 * jnp.sum(rate_rows[:, None] * residual * residual) / key_rows.shape[0]
    gradient = jax.grad(recon_loss)(inner_state)
    updated = jax.tree.map(lambda tensor, slope: tensor - slope, inner_state, gradient)
    return (updated, query_rows + head_forward(updated, query_rows, gain_row, bias_row))

def head_run(inner_state, key_rows, value_rows, query_rows, rate_rows, gain_row, bias_row):

    def advance(state_now, mini_batch):
        return inner_step(state_now, mini_batch, gain_row, bias_row)
    return lax.scan(advance, inner_state, (key_rows, value_rows, query_rows, rate_rows))

def reference(tokens, w_qkv, w_rate, layer_one, layer_two, bias_one, bias_two, inner_gain, inner_bias, inner_rate, out_gain):
    clip_len = CHAIN * TOK_DEV
    blocks = clip_len // MB
    flat_weight = w_qkv.reshape(D, 3 * HEADS * HD)

    def clip_layer(clip_rows):
        projected = jnp.dot(clip_rows, flat_weight, preferred_element_type=jnp.float32).astype(jnp.bfloat16)
        projected = lax.optimization_barrier(projected).reshape(clip_len, 3, HEADS, HD)
        logits = jnp.dot(clip_rows, w_rate, preferred_element_type=jnp.float32)
        rate_vals = inner_rate * jax.nn.sigmoid(logits)

        def arrange(part):
            return jnp.transpose(part.astype(jnp.float32).reshape(blocks, MB, HEADS, HD), (2, 0, 1, 3))
        queries = arrange(projected[:, 0])
        key_rows = arrange(projected[:, 1])
        values = arrange(projected[:, 2])
        rate_blocks = jnp.transpose(rate_vals.reshape(blocks, MB, HEADS), (2, 0, 1))
        run_heads = jax.vmap(head_run)
        _, outputs = run_heads((layer_one, layer_two, bias_one, bias_two), key_rows, values, queries, rate_blocks, inner_gain, inner_bias)
        joined = jnp.transpose(outputs, (1, 2, 0, 3)).reshape(clip_len, D)
        row_mean = lax.optimization_barrier(jnp.mean(joined, -1, keepdims=True))
        centre = joined - row_mean
        variance = lax.optimization_barrier(jnp.mean(centre * centre, -1, keepdims=True))
        return (centre * lax.rsqrt(variance + 1e-05) * out_gain).astype(jnp.bfloat16)
    pieces = lax.map(clip_layer, tokens.reshape(CLIPS, clip_len, D))
    return pieces.reshape(TOKENS, D)
```

```python
import jax
import jax.numpy as jnp
from jax import lax
from jax.experimental import pallas as pl
from jax.experimental.pallas import tpu as pltpu
from jax.sharding import Mesh
from jax.sharding import PartitionSpec as P

D = 3072
HALF = 1536
HD = 64
HID = 256
TOK = 128
MB = 32
CLIP = 1024
STEPS = CLIP // MB
HEADS_DEV = 6
ROWS = 80
C1 = 0.7978845608028654
C2 = 0.044715 * C1
bf16 = jnp.bfloat16
f32 = jnp.float32
NN = (((1,), (0,)), ((), ()))
NT = (((1,), (1,)), ((), ()))
TN = (((0,), (0,)), ((), ()))


def mm(a, b, dims=NN):
    return lax.dot_general(a, b, dims, preferred_element_type=f32)


def gelu(h):
    hh = h * h
    return h * (0.5 + 0.5 * jnp.tanh(h * (C1 + C2 * hh)))


def gelu_and_slope(h):
    hh = h * h
    t = jnp.tanh(h * (C1 + C2 * hh))
    p = 0.5 + 0.5 * t
    return h * p, p + (0.5 * h) * (1.0 - t * t) * (C1 + (3 * C2) * hh)


def pack_kernel(w_ref, wr_ref, out_ref):
    for p in range(8):
        if p >= HEADS_DEV:
            out_ref[p % 4, p // 4] = jnp.zeros((ROWS, 128), bf16)
            continue
        cols = slice(p * HD, (p + 1) * HD)
        q = w_ref[0, :, cols].astype(f32)
        k = w_ref[1, :, cols].astype(f32)
        v = w_ref[2, :, cols].astype(f32)
        gate = wr_ref[p : p + 1, :].astype(f32)
        gate = jnp.concatenate([gate, jnp.zeros((1, 16), f32)], 1)
        gate = jnp.broadcast_to(gate, (16, HD))
        right = jnp.concatenate([q[32:48], gate], 0)
        block = jnp.concatenate(
            [jnp.concatenate([k, v], 1), jnp.concatenate([q[:32], right], 1)], 0
        )
        out_ref[p % 4, p // 4] = block.astype(bf16)


def pack(w, wr):
    return pl.pallas_call(
        pack_kernel,
        out_shape=jax.ShapeDtypeStruct((4, 2, ROWS, 128), bf16),
        name="pack_weights",
    )(w, wr)


def chain_kernel(
    idx,
    rate0,
    own,
    zm,
    zo,
    rm,
    ro,
    lm,
    lo,
    r2m,
    r2o,
    l2m,
    l2o,
    w_hbm,
    A0,
    B0,
    a0,
    b0,
    gain,
    bias,
    o_ref,
    T,
    W,
    WA,
    KV,
    Q,
    RT,
    A,
    B,
    Ab,
    Bb,
    a,
    b,
    hk,
    sem,
):
    head, zi, x, core = idx[0], idx[1], idx[2], idx[3]

    def place(src, z_of, x_of, half):
        row = pl.multiple_of((z_of * 4 + lax.rem(x_of + 8, 4)) * TOK, TOK)
        col = pl.multiple_of(half * HALF, HALF)
        return pltpu.make_async_copy(src, T.at[pl.ds(row, TOK), pl.ds(col, HALF)], sem.at[0])

    me, it = core, 1 - core
    row = pl.multiple_of((zi * 4 + x) * TOK, TOK)
    copies = [
        pltpu.make_async_copy(w_hbm, W, sem.at[1]),
        pltpu.make_async_copy(own, T.at[pl.ds(row, TOK), :], sem.at[0]),
    ]
    for half, z_, r_, l_, r2_, l2_ in ((me, zm, rm, lm, r2m, l2m), (it, zo, ro, lo, r2o, l2o)):
        copies += [
            place(z_, 1 - zi, x, half),
            place(r_.at[0:TOK], zi, x - 1, half),
            place(r_.at[TOK : 2 * TOK], 1 - zi, x - 1, half),
            place(l_.at[0:TOK], zi, x + 1, half),
            place(l_.at[TOK : 2 * TOK], 1 - zi, x + 1, half),
            place(r2_, zi, x + 2, half),
            place(l2_, 1 - zi, x + 2, half),
        ]
    for c in copies:
        c.start()

    gn = gain[pl.ds(head, 1), :]
    bs = bias[pl.ds(head, 1), :]
    A[...] = A0[head]
    Ab[...] = A0[head].astype(bf16)
    Bc = B0[head]
    Bc = Bc - jnp.mean(Bc, 0, keepdims=True)
    B[...] = Bc
    Bb[...] = Bc.astype(bf16)
    a[...] = a0[pl.ds(head, 1), :]
    bb = b0[pl.ds(head, 1), :]
    b[...] = bb - jnp.mean(bb, 1, keepdims=True)

    copies[0].wait()
    WA[:, 0:128] = W[:, 0:48, :].reshape(D, 128)
    X = W[:, 48:80, :]
    lane = lax.broadcasted_iota(jnp.int32, (1, 16, 128), 2)
    sub = lax.broadcasted_iota(jnp.int32, (1, 16, 128), 1)
    gate = X[:, 16:32, :].astype(f32)
    gates = jnp.concatenate(
        [jnp.where(lane == sub + (64 + 16 * j), gate, 0.0) for j in range(3)], 1
    )
    gates = mm(gates.astype(bf16).reshape(D, 128), jnp.ones((128, 128), bf16))
    qa = X[:, 0:16, :].astype(f32)
    qb = jnp.concatenate([qa[:, :, 64:], qa[:, :, :64]], 2)
    qs = jnp.concatenate([X.astype(f32), qb], 1).reshape(D, 128)
    wide = lax.broadcasted_iota(jnp.int32, (1, 128), 1)
    WA[:, 128:256] = jnp.where(wide < 64, qs, gates).astype(bf16)
    for c in copies[1:]:
        c.wait()

    base = rate0[head] * (1.0 / MB)

    def project(i, carry):
        rows = pl.ds(pl.multiple_of(i * 256, 256), 256)
        out = mm(T[rows, :], WA[...])
        KV[rows, :] = out[:, 0:128].astype(bf16)
        Q[rows, :] = out[:, 128:192].astype(bf16)
        RT[rows, :] = base * jax.nn.sigmoid(out[:, 192:256])
        return carry

    lax.fori_loop(0, CLIP // 256, project, 0)

    hk[...] = mm(KV[0:MB, 0:HD], Ab[...]) + a[...]
    g2 = gn * gn

    def answer(rows, q, act, Bv, bv):
        c = mm(act, Bv, NT) + bv
        scale = lax.rsqrt(jnp.mean(c * c, 1, keepdims=True) + 1e-6)
        o_ref[rows, :] = q.astype(f32) + (gn * c * scale + bs)

    def step(t, carry):
        now = pl.ds(pl.multiple_of(t * MB, MB), MB)
        nxt = pl.ds(pl.multiple_of(jnp.minimum(t + 1, STEPS - 1) * MB, MB), MB)
        old = pl.ds(pl.multiple_of(jnp.maximum(t - 1, 0) * MB, MB), MB)
        k = KV[now, 0:HD]
        v = KV[now, HD : 2 * HD]
        kn = KV[nxt, 0:HD]
        qp = Q[old, :]
        w = RT[now, :]
        Av, Bv, av, bv = Ab[...], Bb[...], a[...], b[...]
        act, slope = gelu_and_slope(hk[...])
        act = act.astype(bf16)
        c = mm(act, Bv, NT) + bv
        u = gn * (bs - (v.astype(f32) - k.astype(f32)))
        gc = g2 * c
        s1 = jnp.mean(c * c, 1, keepdims=True)
        s2 = jnp.mean(gc, 1, keepdims=True)
        s3 = jnp.mean(gc * c, 1, keepdims=True)
        s4 = jnp.mean(u * c, 1, keepdims=True)
        s5 = jnp.mean(u, 1, keepdims=True)
        rs = lax.rsqrt(s1 + 1e-6)
        dm = (w * rs) * (gc * rs + (u - (rs * s2 + s5)) - c * (rs * rs * (rs * s3 + s4)))
        dmb = dm.astype(bf16)
        dh = mm(dmb, Bv) * slope
        dhb = dh.astype(bf16)
        gram = (mm(kn, k, NT) + 1.0).astype(bf16)
        hk[...] = mm(kn, Av) + av - mm(gram, dhb)
        answer(old, qp, gelu(mm(qp, Av) + av).astype(bf16), Bv, bv)
        Bn = B[...] - mm(dmb, act, TN)
        B[...] = Bn
        Bb[...] = Bn.astype(bf16)
        b[...] = bv - jnp.sum(dm, 0, keepdims=True)
        An = A[...] - mm(k, dhb, TN)
        A[...] = An
        Ab[...] = An.astype(bf16)
        a[...] = av - jnp.sum(dh, 0, keepdims=True)
        return carry

    lax.fori_loop(0, STEPS, step, 0)
    last = pl.ds(CLIP - MB, MB)
    q = Q[last, :]
    answer(last, q, gelu(mm(q, Ab[...]) + a[...]).astype(bf16), Bb[...], b[...])


def chain(idx, rate0, pieces, w, params):
    hbm = pl.BlockSpec(memory_space=pl.ANY)
    smem = pl.BlockSpec(memory_space=pltpu.SMEM)
    vmem = pl.BlockSpec(memory_space=pltpu.VMEM)
    return pl.pallas_call(
        chain_kernel,
        out_shape=jax.ShapeDtypeStruct((CLIP, HD), f32),
        in_specs=[smem, smem] + [hbm] * (len(pieces) + 1) + [vmem] * len(params),
        out_specs=vmem,
        scratch_shapes=[
            pltpu.VMEM((CLIP, D), bf16),
            pltpu.VMEM((64, ROWS, 128), bf16),
            pltpu.VMEM((D, 256), bf16),
            pltpu.VMEM((CLIP, 2 * HD), bf16),
            pltpu.VMEM((CLIP, HD), bf16),
            pltpu.VMEM((CLIP, HD), f32),
            pltpu.VMEM((HD, HID), f32),
            pltpu.VMEM((HD, HID), f32),
            pltpu.VMEM((HD, HID), bf16),
            pltpu.VMEM((HD, HID), bf16),
            pltpu.VMEM((1, HID), f32),
            pltpu.VMEM((1, HD), f32),
            pltpu.VMEM((MB, HID), f32),
            pltpu.SemaphoreType.DMA((2,)),
        ],
        compiler_params=pltpu.CompilerParams(vmem_limit_bytes=40 * 1024 * 1024),
        name="clip_head",
    )(idx, rate0, *pieces, w, *params)


def ring(x, axis, by):
    size = lax.axis_size(axis)
    return lax.ppermute(x, axis, [(i, (i + by) % size) for i in range(size)])


def local(
    tokens,
    w_qkv,
    w_rate,
    layer_one,
    layer_two,
    bias_one,
    bias_two,
    inner_gain,
    inner_bias,
    inner_rate,
    out_gain,
):
    zi, x, core = (lax.axis_index(n).astype(jnp.int32) for n in ("zi", "x", "core"))
    blocks = pack(jnp.transpose(w_qkv, (1, 0, 2)), jnp.transpose(w_rate))
    blocks = lax.all_to_all(blocks, "x", 0, 0, tiled=True)
    blocks = jnp.transpose(blocks, (1, 0, 2, 3))[None]
    blocks = jnp.broadcast_to(blocks, (8, 2, 4, ROWS, 128)).reshape(16, 4, ROWS, 128)
    weights = lax.all_to_all(blocks, ("zc", "zi"), 0, 0, tiled=True)
    weights = weights.reshape(64, ROWS, 128)

    mine = lax.dynamic_slice(tokens, (0, core * HALF), (TOK, HALF))
    across = ring(mine, "zi", 1)
    pair = jnp.concatenate([mine, across], 0)
    right, left = ring(pair, "x", 1), ring(pair, "x", -1)
    far_own, far_across = ring(right[:TOK], "x", 1), ring(left[TOK:], "x", -1)
    pieces = [tokens]
    for piece in (across, right, left, far_own, far_across):
        pieces += [piece, ring(piece, "core", 1)]

    position = zi * 4 + x
    idx = jnp.stack([jnp.minimum(position, HEADS_DEV - 1), zi, x, core])
    params = (layer_one, layer_two, bias_one, bias_two, inner_gain, inner_bias)
    outs = chain(idx, inner_rate, pieces, weights, params)

    got = lax.all_to_all(outs.reshape(8, TOK, HD), ("zi", "x"), 0, 0, tiled=True)[:HEADS_DEV]
    total = jnp.sum(got, (0, 2))
    offset = got - (total / (HEADS_DEV * HD))[None, :, None]
    squares = jnp.sum(offset * offset, (0, 2))
    stats = jnp.broadcast_to(jnp.stack([total, squares])[None], (8, 2, TOK))
    stats = lax.all_to_all(stats, ("y", "core"), 0, 0, tiled=True)
    mean = jnp.sum(stats[:, 0], 0) / D
    shift = stats[:, 0] / (HEADS_DEV * HD) - mean
    variance = jnp.sum(stats[:, 1] + (HEADS_DEV * HD) * shift * shift, 0) / D
    normed = (got - mean[None, :, None]) * lax.rsqrt(variance + 1e-05)[None, :, None]
    joined = jnp.transpose(normed, (1, 0, 2)).reshape(TOK, HEADS_DEV * HD)
    return (joined * out_gain).astype(bf16)


def solution(mesh):
    fine = Mesh(mesh.devices.reshape(8, 2, 4, 4, 2), ("zc", "zi", "x", "y", "core"))
    ctx, tp = ("zc", "zi", "x"), ("y", "core")
    placed = (
        P(ctx, None),
        P(ctx, None, tp),
        P(ctx, tp),
        P(tp, None, None),
        P(tp, None, None),
        P(tp, None),
        P(tp, None),
        P(tp, None),
        P(tp, None),
        P(tp),
        P(tp),
    )
    return jax.shard_map(local, mesh=fine, in_specs=placed, out_specs=P(ctx, tp), check_vma=False)
```

```python
import jax
import jax.numpy as jnp
from jax import lax
from jax.experimental import pallas as pl
from jax.experimental.pallas import tpu as pltpu
from jax.sharding import Mesh
from jax.sharding import PartitionSpec as P

D = 3072
HALF = 1536
HD = 64
HID = 256
TOK = 128
MB = 32
CLIP = 1024
STEPS = CLIP // MB
HEADS_DEV = 6
SHIFTS = (1, -1, 2)
ROWS = 80
C1 = 0.7978845608028654
C2 = 0.044715 * C1
bf16 = jnp.bfloat16
f32 = jnp.float32
NN = (((1,), (0,)), ((), ()))
NT = (((1,), (1,)), ((), ()))
TN = (((0,), (0,)), ((), ()))


def mm(a, b, dims=NN):
    return lax.dot_general(a, b, dims, preferred_element_type=f32)


def gelu(h):
    hh = h * h
    return h * (0.5 + 0.5 * jnp.tanh(h * (C1 + C2 * hh)))


def gelu_and_slope(h):
    hh = h * h
    t = jnp.tanh(h * (C1 + C2 * hh))
    p = 0.5 + 0.5 * t
    return h * p, p + (0.5 * h) * (1.0 - t * t) * (C1 + (3 * C2) * hh)


def pack_kernel(w_ref, wr_ref, out_ref):
    for p in range(8):
        head = 2 * (p % 4) + p // 4
        if head >= HEADS_DEV:
            out_ref[p % 4, p // 4] = jnp.zeros((ROWS, 128), bf16)
            continue
        cols = slice(head * HD, (head + 1) * HD)
        q = w_ref[0, :, cols].astype(f32)
        k = w_ref[1, :, cols].astype(f32)
        v = w_ref[2, :, cols].astype(f32)
        gate = wr_ref[head : head + 1, :].astype(f32)
        gate = jnp.concatenate([gate, jnp.zeros((1, 16), f32)], 1)
        gate = jnp.broadcast_to(gate, (16, HD))
        right = jnp.concatenate([q[32:48], gate], 0)
        block = jnp.concatenate(
            [jnp.concatenate([k, v], 1), jnp.concatenate([q[:32], right], 1)], 0
        )
        out_ref[p % 4, p // 4] = block.astype(bf16)


def pack(w, wr):
    return pl.pallas_call(
        pack_kernel,
        out_shape=jax.ShapeDtypeStruct((4, 2, ROWS, 128), bf16),
        name="pack_weights",
    )(w, wr)


def chain_kernel(
    idx,
    rate0,
    own,
    z_half,
    r_half,
    l_half,
    f_half,
    z_sibling,
    r_sibling,
    l_sibling,
    f_sibling,
    near,
    other,
    A0_hbm,
    B0_hbm,
    a0_hbm,
    b0_hbm,
    gain_hbm,
    bias_hbm,
    o_ref,
    A0,
    B0,
    a0,
    b0,
    gain,
    bias,
    T,
    W,
    O,
    WA,
    KV,
    Q,
    RT,
    A,
    B,
    Ab,
    Bb,
    a,
    b,
    hk,
    sem,
):
    head, zi, x, core = idx[0], idx[1], idx[2], idx[3]

    def place(src, z_of, x_of, part):
        row = pl.multiple_of((z_of * 4 + lax.rem(x_of + 8, 4)) * TOK, TOK)
        col = pl.multiple_of(part * HALF, HALF)
        return pltpu.make_async_copy(src, T.at[pl.ds(row, TOK), pl.ds(col, HALF)], sem.at[0])

    row = pl.multiple_of((zi * 4 + x) * TOK, TOK)
    copies = [
        pltpu.make_async_copy(near, W.at[:, zi], sem.at[1]),
        pltpu.make_async_copy(other, W.at[:, 1 - zi], sem.at[1]),
        pltpu.make_async_copy(own, T.at[pl.ds(row, TOK), :], sem.at[0]),
    ]
    halves = (z_half, r_half, l_half, f_half)
    siblings = (z_sibling, r_sibling, l_sibling, f_sibling)
    for (across, *pairs), part in ((halves, core), (siblings, 1 - core)):
        copies.append(place(across, 1 - zi, x, part))
        for by, pair in zip(SHIFTS, pairs):
            copies.append(place(pair.at[0:TOK], zi, x - by, part))
            copies.append(place(pair.at[TOK : 2 * TOK], 1 - zi, x - by, part))
    small = [
        pltpu.make_async_copy(A0_hbm.at[head], A0, sem.at[2]),
        pltpu.make_async_copy(B0_hbm.at[head], B0, sem.at[2]),
        pltpu.make_async_copy(a0_hbm, a0, sem.at[2]),
        pltpu.make_async_copy(b0_hbm, b0, sem.at[2]),
        pltpu.make_async_copy(gain_hbm, gain, sem.at[2]),
        pltpu.make_async_copy(bias_hbm, bias, sem.at[2]),
    ]
    for c in small + copies:
        c.start()
    for c in small:
        c.wait()

    gn = gain[pl.ds(head, 1), :]
    bs = bias[pl.ds(head, 1), :]
    A[...] = A0[...]
    Ab[...] = A0[...].astype(bf16)
    Bc = B0[...]
    Bc = Bc - jnp.mean(Bc, 0, keepdims=True)
    B[...] = Bc
    Bb[...] = Bc.astype(bf16)
    a[...] = a0[pl.ds(head, 1), :]
    bb = b0[pl.ds(head, 1), :]
    b[...] = bb - jnp.mean(bb, 1, keepdims=True)

    copies[0].wait()
    copies[1].wait()
    WA[:, 0:128] = W[:, :, :, 0:48, :].reshape(D, 128)
    X = W[:, :, :, 48:80, :].reshape(64, 32, 128)
    lane = lax.broadcasted_iota(jnp.int32, (1, 16, 128), 2)
    sub = lax.broadcasted_iota(jnp.int32, (1, 16, 128), 1)
    gate = X[:, 16:32, :].astype(f32)
    gates = jnp.concatenate(
        [jnp.where(lane == sub + (64 + 16 * j), gate, 0.0) for j in range(3)], 1
    )
    gates = mm(gates.astype(bf16).reshape(D, 128), jnp.ones((128, 128), bf16))
    qa = X[:, 0:16, :].astype(f32)
    qb = jnp.concatenate([qa[:, :, 64:], qa[:, :, :64]], 2)
    qs = jnp.concatenate([X.astype(f32), qb], 1).reshape(D, 128)
    wide = lax.broadcasted_iota(jnp.int32, (1, 128), 1)
    WA[:, 128:256] = jnp.where(wide < 64, qs, gates).astype(bf16)
    for c in copies[2:]:
        c.wait()

    base = rate0[head] * (1.0 / MB)

    def project(i, carry):
        rows = pl.ds(pl.multiple_of(i * 256, 256), 256)
        out = mm(T[rows, :], WA[...])
        KV[rows, :] = out[:, 0:128].astype(bf16)
        Q[rows, :] = out[:, 128:192].astype(bf16)
        RT[rows, :] = base * jax.nn.sigmoid(out[:, 192:256])
        return carry

    lax.fori_loop(0, CLIP // 256, project, 0)

    hk[...] = mm(KV[0:MB, 0:HD], Ab[...]) + a[...]
    g2 = gn * gn

    def answer(rows, q, act, Bv, bv):
        c = mm(act, Bv, NT) + bv
        scale = lax.rsqrt(jnp.mean(c * c, 1, keepdims=True) + 1e-6)
        O[rows, :] = q.astype(f32) + (gn * c * scale + bs)

    def step(t, carry):
        now = pl.ds(pl.multiple_of(t * MB, MB), MB)
        nxt = pl.ds(pl.multiple_of(jnp.minimum(t + 1, STEPS - 1) * MB, MB), MB)
        old = pl.ds(pl.multiple_of(jnp.maximum(t - 1, 0) * MB, MB), MB)
        k = KV[now, 0:HD]
        v = KV[now, HD : 2 * HD]
        kn = KV[nxt, 0:HD]
        qp = Q[old, :]
        w = RT[now, :]
        Av, Bv, av, bv = Ab[...], Bb[...], a[...], b[...]
        act, slope = gelu_and_slope(hk[...])
        act = act.astype(bf16)
        c = mm(act, Bv, NT) + bv
        u = gn * (bs - (v.astype(f32) - k.astype(f32)))
        gc = g2 * c
        s1 = jnp.mean(c * c, 1, keepdims=True)
        s2 = jnp.mean(gc, 1, keepdims=True)
        s3 = jnp.mean(gc * c, 1, keepdims=True)
        s4 = jnp.mean(u * c, 1, keepdims=True)
        s5 = jnp.mean(u, 1, keepdims=True)
        rs = lax.rsqrt(s1 + 1e-6)
        dm = (w * rs) * (gc * rs + (u - (rs * s2 + s5)) - c * (rs * rs * (rs * s3 + s4)))
        dmb = dm.astype(bf16)
        dh = mm(dmb, Bv) * slope
        dhb = dh.astype(bf16)
        gram = (mm(kn, k, NT) + 1.0).astype(bf16)
        hk[...] = mm(kn, Av) + av - mm(gram, dhb)
        answer(old, qp, gelu(mm(qp, Av) + av).astype(bf16), Bv, bv)
        Bn = B[...] - mm(dmb, act, TN)
        B[...] = Bn
        Bb[...] = Bn.astype(bf16)
        b[...] = bv - jnp.sum(dm, 0, keepdims=True)
        An = A[...] - mm(k, dhb, TN)
        A[...] = An
        Ab[...] = An.astype(bf16)
        a[...] = av - jnp.sum(dh, 0, keepdims=True)
        return carry

    lax.fori_loop(0, STEPS, step, 0, unroll=4)
    last = pl.ds(CLIP - MB, MB)
    q = Q[last, :]
    answer(last, q, gelu(mm(q, Ab[...]) + a[...]).astype(bf16), Bb[...], b[...])
    for i in range(8):
        o_ref[i] = jnp.transpose(O[i * TOK : (i + 1) * TOK, :])


def chain(idx, rate0, pieces, weights, params):
    hbm = pl.BlockSpec(memory_space=pl.ANY)
    smem = pl.BlockSpec(memory_space=pltpu.SMEM)
    vmem = pl.BlockSpec(memory_space=pltpu.VMEM)
    return pl.pallas_call(
        chain_kernel,
        out_shape=jax.ShapeDtypeStruct((8, HD, TOK), f32),
        in_specs=[smem, smem] + [hbm] * (len(pieces) + len(weights) + len(params)),
        out_specs=vmem,
        scratch_shapes=[
            pltpu.VMEM((HD, HID), f32),
            pltpu.VMEM((HD, HID), f32),
            pltpu.VMEM((HEADS_DEV, HID), f32),
            pltpu.VMEM((HEADS_DEV, HD), f32),
            pltpu.VMEM((HEADS_DEV, HD), f32),
            pltpu.VMEM((HEADS_DEV, HD), f32),
            pltpu.VMEM((CLIP, D), bf16),
            pltpu.VMEM((8, 2, 4, ROWS, 128), bf16),
            pltpu.VMEM((CLIP, HD), f32),
            pltpu.VMEM((D, 256), bf16),
            pltpu.VMEM((CLIP, 2 * HD), bf16),
            pltpu.VMEM((CLIP, HD), bf16),
            pltpu.VMEM((CLIP, HD), f32),
            pltpu.VMEM((HD, HID), f32),
            pltpu.VMEM((HD, HID), f32),
            pltpu.VMEM((HD, HID), bf16),
            pltpu.VMEM((HD, HID), bf16),
            pltpu.VMEM((1, HID), f32),
            pltpu.VMEM((1, HD), f32),
            pltpu.VMEM((MB, HID), f32),
            pltpu.SemaphoreType.DMA((3,)),
        ],
        compiler_params=pltpu.CompilerParams(vmem_limit_bytes=56 * 1024 * 1024),
        name="clip_head",
    )(idx, rate0, *pieces, *weights, *params)


def ring(x, axis, by):
    size = lax.axis_size(axis)
    return lax.ppermute(x, axis, [(i, (i + by) % size) for i in range(size)])


def to_workers(x, by):
    return lax.ppermute(x, "x", [(i, (i + by) % 4) for i in range(4) if (i + by) % 4 < 3])


def local(
    tokens,
    w_qkv,
    w_rate,
    layer_one,
    layer_two,
    bias_one,
    bias_two,
    inner_gain,
    inner_bias,
    inner_rate,
    out_gain,
):
    zc, zi, x, core = (lax.axis_index(n).astype(jnp.int32) for n in ("zc", "zi", "x", "core"))
    odd = zc % 2
    blocks = pack(jnp.transpose(w_qkv, (1, 0, 2)), jnp.transpose(w_rate))
    blocks = lax.all_to_all(blocks, "x", 0, 0, tiled=True)
    mine = lax.dynamic_slice(tokens, (0, core * HALF), (TOK, HALF))
    across = ring(mine, "zi", 1)
    blocks, across = lax.optimization_barrier((blocks, across))
    keep = lax.dynamic_index_in_dim(blocks, zi, 1, keepdims=False)
    flip = lax.dynamic_index_in_dim(blocks, 1 - zi, 1, keepdims=False)
    blocks = jnp.broadcast_to(jnp.stack([keep, flip])[None], (4, 2, 4, ROWS, 128))
    near = lax.all_to_all(blocks.reshape(8, 4, ROWS, 128), "zc", 0, 0, tiled=True)
    swap = [(i, (i + 1) % 16 if i % 2 else (i - 1) % 16) for i in range(16)]

    pair = jnp.concatenate([mine, across], 0)
    parts = [to_workers(pair, by) for by in SHIFTS]
    other = lax.ppermute(near, ("zc", "zi"), swap)
    parts = [across] + parts
    pieces = [tokens] + parts + [ring(part, "core", 1) for part in parts]

    head = 2 * x + (zi + odd) % 2
    idx = jnp.stack([jnp.minimum(head, HEADS_DEV - 1), zi, x, core])
    params = (layer_one, layer_two, bias_one, bias_two, inner_gain, inner_bias)
    outs = chain(idx, inner_rate, pieces, (near, other), params)

    got = lax.all_to_all(outs, ("zi", "x"), 0, 0, tiled=True)
    even_heads, odd_heads = got[:3], got[4:7]
    got = jnp.stack(
        [jnp.where(odd == 0, even_heads, odd_heads), jnp.where(odd == 0, odd_heads, even_heads)], 1
    ).reshape(HEADS_DEV, HD, TOK)
    total = jnp.sum(got, (0, 1))
    offset = got - (total / (HEADS_DEV * HD))
    squares = jnp.sum(offset * offset, (0, 1))
    stats = jnp.broadcast_to(jnp.stack([total, squares])[None], (8, 2, TOK))
    stats = lax.all_to_all(stats, ("y", "core"), 0, 0, tiled=True)
    mean = jnp.sum(stats[:, 0], 0) / D
    shift = stats[:, 0] / (HEADS_DEV * HD) - mean
    variance = jnp.sum(stats[:, 1] + (HEADS_DEV * HD) * shift * shift, 0) / D
    normed = (got - mean) * lax.rsqrt(variance + 1e-05)
    joined = jnp.transpose(normed.reshape(HEADS_DEV * HD, TOK))
    return (joined * out_gain).astype(bf16)


def solution(mesh):
    fine = Mesh(mesh.devices.reshape(8, 2, 4, 4, 2), ("zc", "zi", "x", "y", "core"))
    ctx, tp = ("zc", "zi", "x"), ("y", "core")
    placed = (
        P(ctx, None),
        P(ctx, None, tp),
        P(ctx, tp),
        P(tp, None, None),
        P(tp, None, None),
        P(tp, None),
        P(tp, None),
        P(tp, None),
        P(tp, None),
        P(tp),
        P(tp),
    )
    return jax.shard_map(local, mesh=fine, in_specs=placed, out_specs=P(ctx, tp), check_vma=False)
```

```python
import jax
import jax.numpy as jnp
from jax import lax
from jax.experimental import pallas as pl
from jax.experimental.pallas import tpu as pltpu
from jax.sharding import Mesh
from jax.sharding import PartitionSpec as P

D = 3072
HALF = 1536
HD = 64
HID = 256
TOK = 128
MB = 32
CLIP = 1024
STEPS = CLIP // MB
HEADS_DEV = 6
SHIFTS = (1, -1, 2)
ROWS = 80
C1 = 0.7978845608028654
C2 = 0.044715 * C1
bf16 = jnp.bfloat16
f32 = jnp.float32
NN = (((1,), (0,)), ((), ()))
NT = (((1,), (1,)), ((), ()))
TN = (((0,), (0,)), ((), ()))


def mm(a, b, dims=NN):
    return lax.dot_general(a, b, dims, preferred_element_type=f32)


def gelu(h):
    hh = h * h
    return h * (0.5 + 0.5 * jnp.tanh(h * (C1 + C2 * hh)))


def gelu_and_slope(h):
    hh = h * h
    t = jnp.tanh(h * (C1 + C2 * hh))
    p = 0.5 + 0.5 * t
    return h * p, p + (0.5 * h) * (1.0 - t * t) * (C1 + (3 * C2) * hh)


def pack_kernel(w_ref, wr_ref, out_ref):
    for p in range(8):
        head = 2 * (p % 4) + p // 4
        if head >= HEADS_DEV:
            out_ref[p % 4, p // 4] = jnp.zeros((ROWS, 128), bf16)
            continue
        cols = slice(head * HD, (head + 1) * HD)
        q = w_ref[0, :, cols].astype(f32)
        k = w_ref[1, :, cols].astype(f32)
        v = w_ref[2, :, cols].astype(f32)
        gate = wr_ref[head : head + 1, :].astype(f32)
        gate = jnp.concatenate([gate, jnp.zeros((1, 16), f32)], 1)
        gate = jnp.broadcast_to(gate, (16, HD))
        right = jnp.concatenate([q[32:48], gate], 0)
        block = jnp.concatenate(
            [jnp.concatenate([k, v], 1), jnp.concatenate([q[:32], right], 1)], 0
        )
        out_ref[p % 4, p // 4] = block.astype(bf16)


def pack(w, wr):
    return pl.pallas_call(
        pack_kernel,
        out_shape=jax.ShapeDtypeStruct((4, 2, ROWS, 128), bf16),
        name="pack_weights",
    )(w, wr)


def chain_kernel(
    idx,
    rate0,
    own,
    z_half,
    r_half,
    l_half,
    f_half,
    z_sibling,
    r_sibling,
    l_sibling,
    f_sibling,
    near,
    other,
    A0_hbm,
    B0_hbm,
    a0_hbm,
    b0_hbm,
    gain_hbm,
    bias_hbm,
    o_ref,
    A0,
    B0,
    a0,
    b0,
    gain,
    bias,
    T,
    W,
    O,
    WA,
    KV,
    Q,
    RT,
    A,
    B,
    Ab,
    Bb,
    a,
    hk,
    sem,
    row_sem,
):
    head, zi, x, core = idx[0], idx[1], idx[2], idx[3]

    def place(src, z_of, x_of, part):
        spot = z_of * 4 + lax.rem(x_of + 8, 4)
        row = pl.multiple_of(spot * TOK, TOK)
        col = pl.multiple_of(part * HALF, HALF)
        there = T.at[pl.ds(row, TOK), pl.ds(col, HALF)]
        return pltpu.make_async_copy(src, there, row_sem.at[spot])

    def wait_rows(spot):
        rows = T.at[pl.ds(pl.multiple_of(spot * TOK, TOK), TOK), :]
        pltpu.make_async_copy(rows, rows, row_sem.at[spot]).wait()

    heavy = [
        pltpu.make_async_copy(near, W.at[:, zi], sem.at[1]),
        pltpu.make_async_copy(other, W.at[:, 1 - zi], sem.at[1]),
    ]
    row = pl.multiple_of((zi * 4 + x) * TOK, TOK)
    copies = [
        pltpu.make_async_copy(own, T.at[pl.ds(row, TOK), :], row_sem.at[zi * 4 + x]),
    ]
    halves = (z_half, r_half, l_half, f_half)
    siblings = (z_sibling, r_sibling, l_sibling, f_sibling)
    for (across, *pairs), part in ((halves, core), (siblings, 1 - core)):
        copies.append(place(across, 1 - zi, x, part))
        for by, pair in zip(SHIFTS, pairs):
            copies.append(place(pair.at[0:TOK], zi, x - by, part))
            copies.append(place(pair.at[TOK : 2 * TOK], 1 - zi, x - by, part))
    small = [
        pltpu.make_async_copy(A0_hbm.at[head], A0, sem.at[0]),
        pltpu.make_async_copy(B0_hbm.at[head], B0, sem.at[0]),
        pltpu.make_async_copy(a0_hbm, a0, sem.at[0]),
        pltpu.make_async_copy(b0_hbm, b0, sem.at[0]),
        pltpu.make_async_copy(gain_hbm, gain, sem.at[0]),
        pltpu.make_async_copy(bias_hbm, bias, sem.at[0]),
    ]
    for c in heavy + small + copies:
        c.start()
    for c in heavy:
        c.wait()
    WA[:, 0:128] = W[:, :, :, 0:48, :].reshape(D, 128)
    X = W[:, :, :, 48:80, :].reshape(64, 32, 128)
    lane = lax.broadcasted_iota(jnp.int32, (1, 16, 128), 2)
    sub = lax.broadcasted_iota(jnp.int32, (1, 16, 128), 1)
    gate = X[:, 16:32, :].astype(f32)
    gates = jnp.concatenate(
        [jnp.where(lane == sub + (64 + 16 * j), gate, 0.0) for j in range(3)], 1
    )
    gates = mm(gates.astype(bf16).reshape(D, 128), jnp.ones((128, 128), bf16))
    qa = X[:, 0:16, :].astype(f32)
    qb = jnp.concatenate([qa[:, :, 64:], qa[:, :, :64]], 2)
    qs = jnp.concatenate([X.astype(f32), qb], 1).reshape(D, 128)
    wide = lax.broadcasted_iota(jnp.int32, (1, 128), 1)
    WA[:, 128:256] = jnp.where(wide < 64, qs, gates).astype(bf16)
    for c in small:
        c.wait()

    gn = gain[pl.ds(head, 1), :]
    bs = bias[pl.ds(head, 1), :]
    A[...] = A0[...]
    Ab[...] = A0[...].astype(bf16)
    Bc = B0[...]
    Bc = Bc - jnp.mean(Bc, 0, keepdims=True)
    B[...] = Bc
    Bb[...] = Bc.astype(bf16)
    a[...] = a0[pl.ds(head, 1), :]
    bb = b0[pl.ds(head, 1), :]
    bb = bb - jnp.mean(bb, 1, keepdims=True)
    gain_col = jnp.transpose(gn)
    square_col = gain_col * gain_col
    base = rate0[head] * (1.0 / MB)

    def project(i, carry):
        for j in range(4):
            wait_rows(4 * i + j)
        rows = pl.ds(pl.multiple_of(i * 512, 512), 512)
        out = mm(T[rows, :], WA[...])
        KV[rows, :] = out[:, 0:128].astype(bf16)
        Q[rows, :] = out[:, 128:192].astype(bf16)
        RT[rows, :] = base * jax.nn.sigmoid(out[:, 192:256])
        return carry

    lax.fori_loop(0, CLIP // 512, project, 0)

    hk[...] = mm(KV[0:MB, 0:HD], Ab[...]) + a[...]

    def answer(rows, q, act, Bv, bv):
        c = mm(act, Bv, NT) + bv
        scale = lax.rsqrt(jnp.mean(c * c, 1, keepdims=True) + 1e-6)
        O[rows, :] = q.astype(f32) + (gn * c * scale + bs)

    def mean(z):
        return jnp.sum(z, 0, keepdims=True) * (1.0 / HD)

    def step(t, carry):
        b_col, b_row = carry
        now = pl.ds(pl.multiple_of(t * MB, MB), MB)
        nxt = pl.ds(pl.multiple_of(jnp.minimum(t + 1, STEPS - 1) * MB, MB), MB)
        old = pl.ds(pl.multiple_of(jnp.maximum(t - 1, 0) * MB, MB), MB)
        k = KV[now, 0:HD]
        v = KV[now, HD : 2 * HD]
        kn = KV[nxt, 0:HD]
        qp = Q[old, :]
        Av, Bv, av = Ab[...], Bb[...], a[...]
        u = jnp.transpose(gn * (bs - (v.astype(f32) - k.astype(f32))))
        w = jnp.transpose(RT[now, :])[0:1, :]
        s5 = mean(u)
        act, slope = gelu_and_slope(hk[...])
        act = act.astype(bf16)
        c = mm(Bv, act, NT) + b_col
        gc = square_col * c
        s1, s2, s3, s4 = mean(c * c), mean(gc), mean(gc * c), mean(u * c)
        rs = lax.rsqrt(s1 + 1e-6)
        wr = w * rs
        dm = gc * (wr * rs) + (u - s5) * wr - wr * (rs * s2) - c * (wr * (rs * rs) * (rs * s3 + s4))
        dmb = dm.astype(bf16)
        dh = mm(dmb, Bv, TN) * slope
        dhb = dh.astype(bf16)
        gram = (mm(kn, k, NT) + 1.0).astype(bf16)
        hk[...] = mm(kn, Av) + av - mm(gram, dhb)
        answer(old, qp, gelu(mm(qp, Av) + av).astype(bf16), Bv, b_row)
        Bn = B[...] - mm(dmb, act)
        B[...] = Bn
        Bb[...] = Bn.astype(bf16)
        An = A[...] - mm(k, dhb, TN)
        A[...] = An
        Ab[...] = An.astype(bf16)
        a[...] = av - jnp.sum(dh, 0, keepdims=True)
        b_col = b_col - jnp.sum(dm, 1, keepdims=True)
        return b_col, jnp.transpose(b_col)

    _, b_row = lax.fori_loop(0, STEPS, step, (jnp.transpose(bb), bb), unroll=8)
    last = pl.ds(CLIP - MB, MB)
    q = Q[last, :]
    answer(last, q, gelu(mm(q, Ab[...]) + a[...]).astype(bf16), Bb[...], b_row)
    for i in range(8):
        o_ref[i] = jnp.transpose(O[i * TOK : (i + 1) * TOK, :])


def chain(idx, rate0, pieces, weights, params):
    hbm = pl.BlockSpec(memory_space=pl.ANY)
    smem = pl.BlockSpec(memory_space=pltpu.SMEM)
    vmem = pl.BlockSpec(memory_space=pltpu.VMEM)
    return pl.pallas_call(
        chain_kernel,
        out_shape=jax.ShapeDtypeStruct((8, HD, TOK), f32),
        in_specs=[smem, smem] + [hbm] * (len(pieces) + len(weights) + len(params)),
        out_specs=vmem,
        scratch_shapes=[
            pltpu.VMEM((HD, HID), f32),
            pltpu.VMEM((HD, HID), f32),
            pltpu.VMEM((HEADS_DEV, HID), f32),
            pltpu.VMEM((HEADS_DEV, HD), f32),
            pltpu.VMEM((HEADS_DEV, HD), f32),
            pltpu.VMEM((HEADS_DEV, HD), f32),
            pltpu.VMEM((CLIP, D), bf16),
            pltpu.VMEM((8, 2, 4, ROWS, 128), bf16),
            pltpu.VMEM((CLIP, HD), f32),
            pltpu.VMEM((D, 256), bf16),
            pltpu.VMEM((CLIP, 2 * HD), bf16),
            pltpu.VMEM((CLIP, HD), bf16),
            pltpu.VMEM((CLIP, HD), f32),
            pltpu.VMEM((HD, HID), f32),
            pltpu.VMEM((HD, HID), f32),
            pltpu.VMEM((HD, HID), bf16),
            pltpu.VMEM((HD, HID), bf16),
            pltpu.VMEM((1, HID), f32),
            pltpu.VMEM((MB, HID), f32),
            pltpu.SemaphoreType.DMA((2,)),
            pltpu.SemaphoreType.DMA((8,)),
        ],
        compiler_params=pltpu.CompilerParams(vmem_limit_bytes=56 * 1024 * 1024),
        name="clip_head",
    )(idx, rate0, *pieces, *weights, *params)


def ring(x, axis, by):
    size = lax.axis_size(axis)
    return lax.ppermute(x, axis, [(i, (i + by) % size) for i in range(size)])


def to_workers(x, by):
    return lax.ppermute(x, "x", [(i, (i + by) % 4) for i in range(4) if (i + by) % 4 < 3])


def local(
    tokens,
    w_qkv,
    w_rate,
    layer_one,
    layer_two,
    bias_one,
    bias_two,
    inner_gain,
    inner_bias,
    inner_rate,
    out_gain,
):
    zc, zi, x, core = (lax.axis_index(n).astype(jnp.int32) for n in ("zc", "zi", "x", "core"))
    odd = zc % 2
    blocks = pack(jnp.transpose(w_qkv, (1, 0, 2)), jnp.transpose(w_rate))
    blocks = lax.all_to_all(blocks, "x", 0, 0, tiled=True)
    mine = lax.dynamic_slice(tokens, (0, core * HALF), (TOK, HALF))
    across = ring(mine, "zi", 1)
    blocks, across = lax.optimization_barrier((blocks, across))
    keep = lax.dynamic_index_in_dim(blocks, zi, 1, keepdims=False)
    flip = lax.dynamic_index_in_dim(blocks, 1 - zi, 1, keepdims=False)
    blocks = jnp.broadcast_to(jnp.stack([keep, flip])[None], (4, 2, 4, ROWS, 128))
    near = lax.all_to_all(blocks.reshape(8, 4, ROWS, 128), "zc", 0, 0, tiled=True)
    swap = [(i, (i + 1) % 16 if i % 2 else (i - 1) % 16) for i in range(16)]

    pair = jnp.concatenate([mine, across], 0)
    parts = [to_workers(pair, by) for by in SHIFTS]
    other = lax.ppermute(near, ("zc", "zi"), swap)
    parts = [across] + parts
    pieces = [tokens] + parts + [ring(part, "core", 1) for part in parts]

    head = 2 * x + (zi + odd) % 2
    idx = jnp.stack([jnp.minimum(head, HEADS_DEV - 1), zi, x, core])
    params = (layer_one, layer_two, bias_one, bias_two, inner_gain, inner_bias)
    outs = chain(idx, inner_rate, pieces, (near, other), params)

    got = lax.all_to_all(outs, ("zi", "x"), 0, 0, tiled=True)
    even_heads, odd_heads = got[:3], got[4:7]
    got = jnp.stack(
        [jnp.where(odd == 0, even_heads, odd_heads), jnp.where(odd == 0, odd_heads, even_heads)], 1
    ).reshape(HEADS_DEV, HD, TOK)
    total = jnp.sum(got, (0, 1))
    offset = got - (total / (HEADS_DEV * HD))
    squares = jnp.sum(offset * offset, (0, 1))
    stats = jnp.broadcast_to(jnp.stack([total, squares])[None], (8, 2, TOK))
    stats = lax.all_to_all(stats, ("y", "core"), 0, 0, tiled=True)
    mean = jnp.sum(stats[:, 0], 0) / D
    shift = stats[:, 0] / (HEADS_DEV * HD) - mean
    variance = jnp.sum(stats[:, 1] + (HEADS_DEV * HD) * shift * shift, 0) / D
    normed = (got - mean) * lax.rsqrt(variance + 1e-05)
    joined = jnp.transpose(normed.reshape(HEADS_DEV * HD, TOK))
    return (joined * out_gain).astype(bf16)


def solution(mesh):
    fine = Mesh(mesh.devices.reshape(8, 2, 4, 4, 2), ("zc", "zi", "x", "y", "core"))
    ctx, tp = ("zc", "zi", "x"), ("y", "core")
    placed = (
        P(ctx, None),
        P(ctx, None, tp),
        P(ctx, tp),
        P(tp, None, None),
        P(tp, None, None),
        P(tp, None),
        P(tp, None),
        P(tp, None),
        P(tp, None),
        P(tp),
        P(tp),
    )
    return jax.shard_map(local, mesh=fine, in_specs=placed, out_specs=P(ctx, tp), check_vma=False)
```

```python
import jax
import jax.numpy as jnp
from jax import lax
from jax.experimental import pallas as pl
from jax.experimental.pallas import tpu as pltpu
from jax.sharding import Mesh
from jax.sharding import PartitionSpec as P

D = 3072
HALF = 1536
HD = 64
HID = 256
TOK = 128
MB = 32
CLIP = 1024
STEPS = CLIP // MB
HEADS_DEV = 6
ROWS = 80
C1 = 0.7978845608028654
C2 = 0.044715 * C1
bf16 = jnp.bfloat16
f32 = jnp.float32
NN = (((1,), (0,)), ((), ()))
NT = (((1,), (1,)), ((), ()))
TN = (((0,), (0,)), ((), ()))


def mm(a, b, dims=NN):
    return lax.dot_general(a, b, dims, preferred_element_type=f32)


def gelu(h):
    hh = h * h
    return h * (0.5 + 0.5 * jnp.tanh(h * (C1 + C2 * hh)))


def gelu_and_slope(h):
    hh = h * h
    t = jnp.tanh(h * (C1 + C2 * hh))
    p = 0.5 + 0.5 * t
    return h * p, p + (0.5 * h) * (1.0 - t * t) * (C1 + (3 * C2) * hh)


def pack_kernel(w_ref, wr_ref, out_ref):
    for p in range(8):
        head = 2 * (p % 4) + p // 4
        if head >= HEADS_DEV:
            out_ref[p % 4, p // 4] = jnp.zeros((ROWS, 128), bf16)
            continue
        cols = slice(head * HD, (head + 1) * HD)
        q = w_ref[0, :, cols].astype(f32)
        k = w_ref[1, :, cols].astype(f32)
        v = w_ref[2, :, cols].astype(f32)
        gate = wr_ref[head : head + 1, :].astype(f32)
        gate = jnp.concatenate([gate, jnp.zeros((1, 16), f32)], 1)
        gate = jnp.broadcast_to(gate, (16, HD))
        right = jnp.concatenate([q[32:48], gate], 0)
        block = jnp.concatenate(
            [jnp.concatenate([k, v], 1), jnp.concatenate([q[:32], right], 1)], 0
        )
        out_ref[p % 4, p // 4] = block.astype(bf16)


def pack(w, wr):
    return pl.pallas_call(
        pack_kernel,
        out_shape=jax.ShapeDtypeStruct((4, 2, ROWS, 128), bf16),
        name="pack_weights",
    )(w, wr)


def chain_kernel(
    idx,
    rate0,
    own,
    z_half,
    r_half,
    l_half,
    f_half,
    g_half,
    z_sibling,
    r_sibling,
    l_sibling,
    f_sibling,
    g_sibling,
    near,
    other,
    A0_hbm,
    B0_hbm,
    a0_hbm,
    b0_hbm,
    gain_hbm,
    bias_hbm,
    o_ref,
    A0,
    B0,
    a0,
    b0,
    gain,
    bias,
    T,
    W,
    O,
    WA,
    KV,
    Q,
    RT,
    A,
    B,
    Ab,
    Bb,
    a,
    hk,
    sem,
    row_sem,
):
    head, zi, x, core = idx[0], idx[1], idx[2], idx[3]

    def place(src, z_of, x_of, part):
        spot = z_of * 4 + lax.rem(x_of + 8, 4)
        row = pl.multiple_of(spot * TOK, TOK)
        col = pl.multiple_of(part * HALF, HALF)
        there = T.at[pl.ds(row, TOK), pl.ds(col, HALF)]
        return pltpu.make_async_copy(src, there, row_sem.at[spot])

    def wait_rows(spot):
        rows = T.at[pl.ds(pl.multiple_of(spot * TOK, TOK), TOK), :]
        pltpu.make_async_copy(rows, rows, row_sem.at[spot]).wait()

    heavy = [
        pltpu.make_async_copy(near, W.at[:, zi], sem.at[1]),
        pltpu.make_async_copy(other, W.at[:, 1 - zi], sem.at[1]),
    ]
    row = pl.multiple_of((zi * 4 + x) * TOK, TOK)
    copies = [
        pltpu.make_async_copy(own, T.at[pl.ds(row, TOK), :], row_sem.at[zi * 4 + x]),
    ]
    halves = (z_half, r_half, l_half, f_half, g_half)
    siblings = (z_sibling, r_sibling, l_sibling, f_sibling, g_sibling)
    for (across, right, left, far_own, far_across), part in ((halves, core), (siblings, 1 - core)):
        copies.append(place(across, 1 - zi, x, part))
        for by, pair in ((1, right), (-1, left)):
            copies.append(place(pair.at[0:TOK], zi, x - by, part))
            copies.append(place(pair.at[TOK : 2 * TOK], 1 - zi, x - by, part))
        copies.append(place(far_own, zi, x + 2, part))
        copies.append(place(far_across, 1 - zi, x + 2, part))
    small = [
        pltpu.make_async_copy(A0_hbm.at[head], A0, sem.at[0]),
        pltpu.make_async_copy(B0_hbm.at[head], B0, sem.at[0]),
        pltpu.make_async_copy(a0_hbm, a0, sem.at[0]),
        pltpu.make_async_copy(b0_hbm, b0, sem.at[0]),
        pltpu.make_async_copy(gain_hbm, gain, sem.at[0]),
        pltpu.make_async_copy(bias_hbm, bias, sem.at[0]),
    ]
    for c in heavy + small + copies:
        c.start()
    for c in heavy:
        c.wait()
    WA[:, 0:128] = W[:, :, :, 0:48, :].reshape(D, 128)
    X = W[:, :, :, 48:80, :].reshape(64, 32, 128)
    lane = lax.broadcasted_iota(jnp.int32, (1, 16, 128), 2)
    sub = lax.broadcasted_iota(jnp.int32, (1, 16, 128), 1)
    gate = X[:, 16:32, :].astype(f32)
    gates = jnp.concatenate(
        [jnp.where(lane == sub + (64 + 16 * j), gate, 0.0) for j in range(3)], 1
    )
    gates = mm(gates.astype(bf16).reshape(D, 128), jnp.ones((128, 128), bf16))
    qa = X[:, 0:16, :].astype(f32)
    qb = jnp.concatenate([qa[:, :, 64:], qa[:, :, :64]], 2)
    qs = jnp.concatenate([X.astype(f32), qb], 1).reshape(D, 128)
    wide = lax.broadcasted_iota(jnp.int32, (1, 128), 1)
    WA[:, 128:256] = jnp.where(wide < 64, qs, gates).astype(bf16)
    for c in small:
        c.wait()

    gn = gain[pl.ds(head, 1), :]
    bs = bias[pl.ds(head, 1), :]
    A[...] = A0[...]
    Ab[...] = A0[...].astype(bf16)
    Bc = B0[...]
    Bc = Bc - jnp.mean(Bc, 0, keepdims=True)
    B[...] = Bc
    Bb[...] = Bc.astype(bf16)
    a[...] = a0[pl.ds(head, 1), :]
    bb = b0[pl.ds(head, 1), :]
    bb = bb - jnp.mean(bb, 1, keepdims=True)
    gain_col = jnp.transpose(gn)
    square_col = gain_col * gain_col
    base = rate0[head] * (1.0 / MB)

    def project(i, carry):
        for j in range(4):
            wait_rows(4 * i + j)
        rows = pl.ds(pl.multiple_of(i * 512, 512), 512)
        out = mm(T[rows, :], WA[...])
        KV[rows, :] = out[:, 0:128].astype(bf16)
        Q[rows, :] = out[:, 128:192].astype(bf16)
        RT[rows, :] = base * jax.nn.sigmoid(out[:, 192:256])
        return carry

    lax.fori_loop(0, CLIP // 512, project, 0)

    hk[...] = mm(KV[0:MB, 0:HD], Ab[...]) + a[...]

    def answer(rows, q, act, Bv, bv):
        c = mm(act, Bv, NT) + bv
        scale = lax.rsqrt(jnp.mean(c * c, 1, keepdims=True) + 1e-6)
        O[rows, :] = q.astype(f32) + (gn * c * scale + bs)

    def mean(z):
        return jnp.sum(z, 0, keepdims=True) * (1.0 / HD)

    def step(t, carry):
        b_col, b_row = carry
        now = pl.ds(pl.multiple_of(t * MB, MB), MB)
        nxt = pl.ds(pl.multiple_of(jnp.minimum(t + 1, STEPS - 1) * MB, MB), MB)
        old = pl.ds(pl.multiple_of(jnp.maximum(t - 1, 0) * MB, MB), MB)
        k = KV[now, 0:HD]
        v = KV[now, HD : 2 * HD]
        kn = KV[nxt, 0:HD]
        qp = Q[old, :]
        Av, Bv, av = Ab[...], Bb[...], a[...]
        u = jnp.transpose(gn * (bs - (v.astype(f32) - k.astype(f32))))
        w = jnp.transpose(RT[now, :])[0:1, :]
        s5 = mean(u)
        act, slope = gelu_and_slope(hk[...])
        act = act.astype(bf16)
        c = mm(Bv, act, NT) + b_col
        gc = square_col * c
        s1, s2, s3, s4 = mean(c * c), mean(gc), mean(gc * c), mean(u * c)
        rs = lax.rsqrt(s1 + 1e-6)
        wr = w * rs
        dm = gc * (wr * rs) + (u - s5) * wr - wr * (rs * s2) - c * (wr * (rs * rs) * (rs * s3 + s4))
        dmb = dm.astype(bf16)
        dh = mm(dmb, Bv, TN) * slope
        dhb = dh.astype(bf16)
        gram = (mm(kn, k, NT) + 1.0).astype(bf16)
        hk[...] = mm(kn, Av) + av - mm(gram, dhb)
        answer(old, qp, gelu(mm(qp, Av) + av).astype(bf16), Bv, b_row)
        Bn = B[...] - mm(dmb, act)
        B[...] = Bn
        Bb[...] = Bn.astype(bf16)
        An = A[...] - mm(k, dhb, TN)
        A[...] = An
        Ab[...] = An.astype(bf16)
        a[...] = av - jnp.sum(dh, 0, keepdims=True)
        b_col = b_col - jnp.sum(dm, 1, keepdims=True)
        return b_col, jnp.transpose(b_col)

    _, b_row = lax.fori_loop(0, STEPS, step, (jnp.transpose(bb), bb), unroll=8)
    last = pl.ds(CLIP - MB, MB)
    q = Q[last, :]
    answer(last, q, gelu(mm(q, Ab[...]) + a[...]).astype(bf16), Bb[...], b_row)
    for i in range(8):
        o_ref[i] = jnp.transpose(O[i * TOK : (i + 1) * TOK, :])


def chain(idx, rate0, pieces, weights, params):
    hbm = pl.BlockSpec(memory_space=pl.ANY)
    smem = pl.BlockSpec(memory_space=pltpu.SMEM)
    vmem = pl.BlockSpec(memory_space=pltpu.VMEM)
    return pl.pallas_call(
        chain_kernel,
        out_shape=jax.ShapeDtypeStruct((8, HD, TOK), f32),
        in_specs=[smem, smem] + [hbm] * (len(pieces) + len(weights) + len(params)),
        out_specs=vmem,
        scratch_shapes=[
            pltpu.VMEM((HD, HID), f32),
            pltpu.VMEM((HD, HID), f32),
            pltpu.VMEM((HEADS_DEV, HID), f32),
            pltpu.VMEM((HEADS_DEV, HD), f32),
            pltpu.VMEM((HEADS_DEV, HD), f32),
            pltpu.VMEM((HEADS_DEV, HD), f32),
            pltpu.VMEM((CLIP, D), bf16),
            pltpu.VMEM((8, 2, 4, ROWS, 128), bf16),
            pltpu.VMEM((CLIP, HD), f32),
            pltpu.VMEM((D, 256), bf16),
            pltpu.VMEM((CLIP, 2 * HD), bf16),
            pltpu.VMEM((CLIP, HD), bf16),
            pltpu.VMEM((CLIP, HD), f32),
            pltpu.VMEM((HD, HID), f32),
            pltpu.VMEM((HD, HID), f32),
            pltpu.VMEM((HD, HID), bf16),
            pltpu.VMEM((HD, HID), bf16),
            pltpu.VMEM((1, HID), f32),
            pltpu.VMEM((MB, HID), f32),
            pltpu.SemaphoreType.DMA((2,)),
            pltpu.SemaphoreType.DMA((8,)),
        ],
        compiler_params=pltpu.CompilerParams(vmem_limit_bytes=56 * 1024 * 1024),
        name="clip_head",
    )(idx, rate0, *pieces, *weights, *params)


def ring(x, axis, by):
    size = lax.axis_size(axis)
    return lax.ppermute(x, axis, [(i, (i + by) % size) for i in range(size)])


def local(
    tokens,
    w_qkv,
    w_rate,
    layer_one,
    layer_two,
    bias_one,
    bias_two,
    inner_gain,
    inner_bias,
    inner_rate,
    out_gain,
):
    zc, zi, x, core = (lax.axis_index(n).astype(jnp.int32) for n in ("zc", "zi", "x", "core"))
    odd = zc % 2
    blocks = pack(jnp.transpose(w_qkv, (1, 0, 2)), jnp.transpose(w_rate))
    blocks = lax.all_to_all(blocks, "x", 0, 0, tiled=True)
    mine = lax.dynamic_slice(tokens, (0, core * HALF), (TOK, HALF))
    across = ring(mine, "zi", 1)
    blocks, across = lax.optimization_barrier((blocks, across))
    keep = lax.dynamic_index_in_dim(blocks, zi, 1, keepdims=False)
    flip = lax.dynamic_index_in_dim(blocks, 1 - zi, 1, keepdims=False)
    blocks = jnp.broadcast_to(jnp.stack([keep, flip])[None], (4, 2, 4, ROWS, 128))
    near = lax.all_to_all(blocks.reshape(8, 4, ROWS, 128), "zc", 0, 0, tiled=True)
    swap = [(i, (i + 1) % 16 if i % 2 else (i - 1) % 16) for i in range(16)]

    pair = jnp.concatenate([mine, across], 0)
    right, left = ring(pair, "x", 1), ring(pair, "x", -1)
    far_own, far_across = ring(right[:TOK], "x", 1), ring(left[TOK:], "x", -1)
    other = lax.ppermute(near, ("zc", "zi"), swap)
    parts = [across, right, left, far_own, far_across]
    pieces = [tokens] + parts + [ring(part, "core", 1) for part in parts]

    head = 2 * x + (zi + odd) % 2
    idx = jnp.stack([jnp.minimum(head, HEADS_DEV - 1), zi, x, core])
    params = (layer_one, layer_two, bias_one, bias_two, inner_gain, inner_bias)
    outs = chain(idx, inner_rate, pieces, (near, other), params)

    got = lax.all_to_all(outs, ("zi", "x"), 0, 0, tiled=True)
    even_heads, odd_heads = got[:3], got[4:7]
    got = jnp.stack(
        [jnp.where(odd == 0, even_heads, odd_heads), jnp.where(odd == 0, odd_heads, even_heads)], 1
    ).reshape(HEADS_DEV, HD, TOK)
    total = jnp.sum(got, (0, 1))
    offset = got - (total / (HEADS_DEV * HD))
    squares = jnp.sum(offset * offset, (0, 1))
    stats = jnp.broadcast_to(jnp.stack([total, squares])[None], (8, 2, TOK))
    stats = lax.all_to_all(stats, ("y", "core"), 0, 0, tiled=True)
    mean = jnp.sum(stats[:, 0], 0) / D
    shift = stats[:, 0] / (HEADS_DEV * HD) - mean
    variance = jnp.sum(stats[:, 1] + (HEADS_DEV * HD) * shift * shift, 0) / D
    normed = (got - mean) * lax.rsqrt(variance + 1e-05)
    joined = jnp.transpose(normed.reshape(HEADS_DEV * HD, TOK))
    return (joined * out_gain).astype(bf16)


def solution(mesh):
    fine = Mesh(mesh.devices.reshape(8, 2, 4, 4, 2), ("zc", "zi", "x", "y", "core"))
    ctx, tp = ("zc", "zi", "x"), ("y", "core")
    placed = (
        P(ctx, None),
        P(ctx, None, tp),
        P(ctx, tp),
        P(tp, None, None),
        P(tp, None, None),
        P(tp, None),
        P(tp, None),
        P(tp, None),
        P(tp, None),
        P(tp),
        P(tp),
    )
    return jax.shard_map(local, mesh=fine, in_specs=placed, out_specs=P(ctx, tp), check_vma=False)
```

```python
import jax
import jax.numpy as jnp
from jax import lax
from jax.experimental import pallas as pl
from jax.experimental.pallas import tpu as pltpu
from jax.sharding import Mesh
from jax.sharding import PartitionSpec as P

D = 3072
HALF = 1536
HD = 64
HID = 256
TOK = 128
MB = 32
CLIP = 1024
STEPS = CLIP // MB
HEADS_DEV = 6
ROWS = 80
SLAB = 304
C1 = 0.7978845608028654
C2 = 0.044715 * C1
bf16 = jnp.bfloat16
f32 = jnp.float32
NN = (((1,), (0,)), ((), ()))
NT = (((1,), (1,)), ((), ()))
TN = (((0,), (0,)), ((), ()))


def mm(a, b, dims=NN):
    return lax.dot_general(a, b, dims, preferred_element_type=f32)


def gelu(h):
    hh = h * h
    return h * (0.5 + 0.5 * jnp.tanh(h * (C1 + C2 * hh)))


def gelu_and_slope(h):
    hh = h * h
    t = jnp.tanh(h * (C1 + C2 * hh))
    p = 0.5 + 0.5 * t
    return h * p, p + (0.5 * h) * (1.0 - t * t) * (C1 + (3 * C2) * hh)


def pack_kernel(w_ref, wr_ref, out_ref):
    for p in range(8):
        head = 2 * (p % 4) + p // 4
        if head >= HEADS_DEV:
            out_ref[p % 4, p // 4] = jnp.zeros((ROWS, 128), bf16)
            continue
        cols = slice(head * HD, (head + 1) * HD)
        q = w_ref[0, :, cols].astype(f32)
        k = w_ref[1, :, cols].astype(f32)
        v = w_ref[2, :, cols].astype(f32)
        gate = wr_ref[head : head + 1, :].astype(f32)
        gate = jnp.concatenate([gate, jnp.zeros((1, 80), f32)], 1)
        queries = jnp.concatenate([q[:24], q[24:]], 1)
        block = jnp.concatenate(
            [jnp.concatenate([k, v], 1), queries, jnp.broadcast_to(gate, (8, 128))], 0
        )
        out_ref[p % 4, p // 4] = block.astype(bf16)


def pack(w, wr):
    return pl.pallas_call(
        pack_kernel,
        out_shape=jax.ShapeDtypeStruct((4, 2, ROWS, 128), bf16),
        name="pack_weights",
    )(w, wr)


def chain_kernel(
    idx,
    rate0,
    own,
    z_half,
    r_half,
    l_half,
    f_half,
    g_half,
    z_sibling,
    r_sibling,
    l_sibling,
    f_sibling,
    g_sibling,
    near,
    other,
    A0_hbm,
    B0_hbm,
    a0_hbm,
    b0_hbm,
    gain_hbm,
    bias_hbm,
    o_ref,
    A0,
    B0,
    a0,
    b0,
    gain,
    bias,
    T,
    W,
    O,
    WA,
    KV,
    Q,
    RT,
    A,
    B,
    Ab,
    Bb,
    a,
    hk,
    sem,
    row_sem,
):
    head, zi, x, core = idx[0], idx[1], idx[2], idx[3]

    def place(src, z_of, x_of, part):
        spot = z_of * 4 + lax.rem(x_of + 8, 4)
        row = pl.multiple_of(spot * TOK, TOK)
        col = pl.multiple_of(part * HALF, HALF)
        there = T.at[pl.ds(row, TOK), pl.ds(col, HALF)]
        return pltpu.make_async_copy(src, there, row_sem.at[spot])

    def wait_rows(spot):
        rows = T.at[pl.ds(pl.multiple_of(spot * TOK, TOK), TOK), :]
        pltpu.make_async_copy(rows, rows, row_sem.at[spot]).wait()

    heavy = [
        pltpu.make_async_copy(near, W.at[:, zi], sem.at[1]),
        pltpu.make_async_copy(other, W.at[:, 1 - zi], sem.at[1]),
    ]
    row = pl.multiple_of((zi * 4 + x) * TOK, TOK)
    copies = [
        pltpu.make_async_copy(own, T.at[pl.ds(row, TOK), :], row_sem.at[zi * 4 + x]),
    ]
    halves = (z_half, r_half, l_half, f_half, g_half)
    siblings = (z_sibling, r_sibling, l_sibling, f_sibling, g_sibling)
    for (across, right, left, far_own, far_across), part in ((halves, core), (siblings, 1 - core)):
        copies.append(place(across, 1 - zi, x, part))
        for by, pair in ((1, right), (-1, left)):
            copies.append(place(pair.at[0:TOK], zi, x - by, part))
            copies.append(place(pair.at[TOK : 2 * TOK], 1 - zi, x - by, part))
        copies.append(place(far_own, zi, x + 2, part))
        copies.append(place(far_across, 1 - zi, x + 2, part))
    small = [
        pltpu.make_async_copy(A0_hbm.at[head], A0, sem.at[0]),
        pltpu.make_async_copy(B0_hbm.at[head], B0, sem.at[0]),
        pltpu.make_async_copy(a0_hbm, a0, sem.at[0]),
        pltpu.make_async_copy(b0_hbm, b0, sem.at[0]),
        pltpu.make_async_copy(gain_hbm, gain, sem.at[0]),
        pltpu.make_async_copy(bias_hbm, bias, sem.at[0]),
    ]
    for c in heavy + small + copies:
        c.start()
    for c in heavy:
        c.wait()
    blocks = W[...].reshape(16, SLAB, 128)
    WA[:, 0:128] = blocks[:, 0:192, :].reshape(D, 128)
    X = blocks[:, 192:288, :].astype(f32)
    G = blocks[:, 288:304, :].astype(f32)
    lane = lax.broadcasted_iota(jnp.int32, (1, 48, 128), 2)
    sub = lax.broadcasted_iota(jnp.int32, (1, 48, 128), 1)
    gates, qs = [], []
    for i in range(4):
        gates.append(jnp.where(lane == sub, G[:, 4 * i : 4 * i + 1, :], 0.0))
        q = X[:, 24 * i : 24 * i + 24, :]
        qs += [q, jnp.concatenate([q[:, :, 64:], q[:, :, :64]], 2)]
    gates = jnp.concatenate(gates, 1).astype(bf16).reshape(D, 128)
    gates = mm(gates, jnp.ones((128, 128), bf16))
    qs = jnp.concatenate(qs, 1).reshape(D, 128)
    wide = lax.broadcasted_iota(jnp.int32, (1, 128), 1)
    WA[:, 128:256] = jnp.where(wide < 64, qs, gates).astype(bf16)
    for c in small:
        c.wait()

    gn = gain[pl.ds(head, 1), :]
    bs = bias[pl.ds(head, 1), :]
    A[...] = A0[...]
    Ab[...] = A0[...].astype(bf16)
    Bc = B0[...]
    Bc = Bc - jnp.mean(Bc, 0, keepdims=True)
    B[...] = Bc
    Bb[...] = Bc.astype(bf16)
    a[...] = a0[pl.ds(head, 1), :]
    bb = b0[pl.ds(head, 1), :]
    bb = bb - jnp.mean(bb, 1, keepdims=True)
    gain_col = jnp.transpose(gn)
    square_col = gain_col * gain_col
    base = rate0[head] * (1.0 / MB)

    def project(i, carry):
        for j in range(4):
            wait_rows(4 * i + j)
        rows = pl.ds(pl.multiple_of(i * 512, 512), 512)
        out = mm(T[rows, :], WA[...])
        KV[rows, :] = out[:, 0:128].astype(bf16)
        Q[rows, :] = out[:, 128:192].astype(bf16)
        RT[rows, :] = base * jax.nn.sigmoid(out[:, 192:256])
        return carry

    lax.fori_loop(0, CLIP // 512, project, 0)

    hk[...] = mm(KV[0:MB, 0:HD], Ab[...]) + a[...]

    def answer(rows, q, act, Bv, bv):
        c = mm(act, Bv, NT) + bv
        scale = lax.rsqrt(jnp.mean(c * c, 1, keepdims=True) + 1e-6)
        O[rows, :] = q.astype(f32) + (gn * c * scale + bs)

    def mean(z):
        return jnp.sum(z, 0, keepdims=True) * (1.0 / HD)

    def step(t, carry):
        b_col, b_row = carry
        now = pl.ds(t * MB, MB)
        nxt = pl.ds(min(t + 1, STEPS - 1) * MB, MB)
        old = pl.ds(max(t - 1, 0) * MB, MB)
        k = KV[now, 0:HD]
        v = KV[now, HD : 2 * HD]
        kn = KV[nxt, 0:HD]
        qp = Q[old, :]
        Av, Bv, av = Ab[...], Bb[...], a[...]
        u = jnp.transpose(gn * (bs - (v.astype(f32) - k.astype(f32))))
        w = jnp.transpose(RT[now, :])[0:1, :]
        s5 = mean(u)
        act, slope = gelu_and_slope(hk[...])
        act = act.astype(bf16)
        c = mm(Bv, act, NT) + b_col
        gc = square_col * c
        s1, s2, s3, s4 = mean(c * c), mean(gc), mean(gc * c), mean(u * c)
        rs = lax.rsqrt(s1 + 1e-6)
        wr = w * rs
        dm = gc * (wr * rs) + (u - s5) * wr - wr * (rs * s2) - c * (wr * (rs * rs) * (rs * s3 + s4))
        dmb = dm.astype(bf16)
        dh = mm(dmb, Bv, TN) * slope
        dhb = dh.astype(bf16)
        if t < STEPS - 1:
            gram = (mm(kn, k, NT) + 1.0).astype(bf16)
            hk[...] = mm(kn, Av) + av - mm(gram, dhb)
        if t > 0:
            answer(old, qp, gelu(mm(qp, Av) + av).astype(bf16), Bv, b_row)
        Bn = B[...] - mm(dmb, act)
        B[...] = Bn
        Bb[...] = Bn.astype(bf16)
        An = A[...] - mm(k, dhb, TN)
        A[...] = An
        Ab[...] = An.astype(bf16)
        a[...] = av - jnp.sum(dh, 0, keepdims=True)
        b_col = b_col - jnp.sum(dm, 1, keepdims=True)
        return b_col, jnp.transpose(b_col)

    state = (jnp.transpose(bb), bb)
    for t in range(STEPS):
        state = step(t, state)
    _, b_row = state
    last = pl.ds(CLIP - MB, MB)
    q = Q[last, :]
    answer(last, q, gelu(mm(q, Ab[...]) + a[...]).astype(bf16), Bb[...], b_row)
    for i in range(8):
        o_ref[i] = jnp.transpose(O[i * TOK : (i + 1) * TOK, :])


def chain(idx, rate0, pieces, weights, params):
    hbm = pl.BlockSpec(memory_space=pl.ANY)
    smem = pl.BlockSpec(memory_space=pltpu.SMEM)
    vmem = pl.BlockSpec(memory_space=pltpu.VMEM)
    return pl.pallas_call(
        chain_kernel,
        out_shape=jax.ShapeDtypeStruct((8, HD, TOK), f32),
        in_specs=[smem, smem] + [hbm] * (len(pieces) + len(weights) + len(params)),
        out_specs=vmem,
        scratch_shapes=[
            pltpu.VMEM((HD, HID), f32),
            pltpu.VMEM((HD, HID), f32),
            pltpu.VMEM((HEADS_DEV, HID), f32),
            pltpu.VMEM((HEADS_DEV, HD), f32),
            pltpu.VMEM((HEADS_DEV, HD), f32),
            pltpu.VMEM((HEADS_DEV, HD), f32),
            pltpu.VMEM((CLIP, D), bf16),
            pltpu.VMEM((8, 2, SLAB, 128), bf16),
            pltpu.VMEM((CLIP, HD), f32),
            pltpu.VMEM((D, 256), bf16),
            pltpu.VMEM((CLIP, 2 * HD), bf16),
            pltpu.VMEM((CLIP, HD), bf16),
            pltpu.VMEM((CLIP, HD), f32),
            pltpu.VMEM((HD, HID), f32),
            pltpu.VMEM((HD, HID), f32),
            pltpu.VMEM((HD, HID), bf16),
            pltpu.VMEM((HD, HID), bf16),
            pltpu.VMEM((1, HID), f32),
            pltpu.VMEM((MB, HID), f32),
            pltpu.SemaphoreType.DMA((2,)),
            pltpu.SemaphoreType.DMA((8,)),
        ],
        compiler_params=pltpu.CompilerParams(vmem_limit_bytes=56 * 1024 * 1024),
        name="clip_head",
    )(idx, rate0, *pieces, *weights, *params)


def turn_kernel(x_ref, o_ref):
    o_ref[...] = jnp.transpose(x_ref[...].reshape(HEADS_DEV * HD, TOK))


def by_token(x):
    return pl.pallas_call(
        turn_kernel,
        out_shape=jax.ShapeDtypeStruct((TOK, HEADS_DEV * HD), f32),
        name="by_token",
    )(x)


def ring(x, axis, by):
    size = lax.axis_size(axis)
    return lax.ppermute(x, axis, [(i, (i + by) % size) for i in range(size)])


def local(
    tokens,
    w_qkv,
    w_rate,
    layer_one,
    layer_two,
    bias_one,
    bias_two,
    inner_gain,
    inner_bias,
    inner_rate,
    out_gain,
):
    zc, zi, x, core = (lax.axis_index(n).astype(jnp.int32) for n in ("zc", "zi", "x", "core"))
    odd = zc % 2
    blocks = pack(jnp.transpose(w_qkv, (1, 0, 2)), jnp.transpose(w_rate))
    blocks = lax.all_to_all(blocks.reshape(4, 2 * ROWS, 128), "x", 0, 0, tiled=True)
    blocks = blocks.reshape(4, 2, ROWS, 128)
    mine = lax.dynamic_slice(tokens, (0, core * HALF), (TOK, HALF))
    across = ring(mine, "zi", 1)
    blocks, across = lax.optimization_barrier((blocks, across))
    def gathered(which):
        block = lax.dynamic_index_in_dim(blocks, which, 1, keepdims=False)
        parts = block[:, :48], block[:, 48:72], block[:, 72:76]
        return jnp.concatenate([part.reshape(-1, 128) for part in parts], 0)

    both = jnp.stack([gathered(zi), gathered(1 - zi)])[None]
    both = jnp.broadcast_to(both, (4, 2, SLAB, 128)).reshape(8, SLAB, 128)
    near = lax.all_to_all(both, "zc", 0, 0, tiled=True)
    swap = [(i, (i + 1) % 16 if i % 2 else (i - 1) % 16) for i in range(16)]

    pair = jnp.concatenate([mine, across], 0)
    right, left = ring(pair, "x", 1), ring(pair, "x", -1)
    far_own, far_across = ring(right[:TOK], "x", 1), ring(left[TOK:], "x", -1)
    other = lax.ppermute(near, ("zc", "zi"), swap)
    parts = [across, right, left, far_own, far_across]
    pieces = [tokens] + parts + [ring(part, "core", 1) for part in parts]

    head = 2 * x + (zi + odd) % 2
    idx = jnp.stack([jnp.minimum(head, HEADS_DEV - 1), zi, x, core])
    params = (layer_one, layer_two, bias_one, bias_two, inner_gain, inner_bias)
    outs = chain(idx, inner_rate, pieces, (near, other), params)

    got = lax.all_to_all(outs, ("zi", "x"), 0, 0, tiled=True)
    even_heads, odd_heads = got[:3], got[4:7]
    got = jnp.stack(
        [jnp.where(odd == 0, even_heads, odd_heads), jnp.where(odd == 0, odd_heads, even_heads)], 1
    ).reshape(HEADS_DEV, HD, TOK)
    total = jnp.sum(got, (0, 1))
    offset = got - (total / (HEADS_DEV * HD))
    squares = jnp.sum(offset * offset, (0, 1))
    stats = jnp.broadcast_to(jnp.stack([total, squares])[None], (8, 2, TOK))
    joined = by_token(got)
    stats = lax.all_to_all(stats, ("y", "core"), 0, 0, tiled=True)
    mean = jnp.sum(stats[:, 0], 0) / D
    shift = stats[:, 0] / (HEADS_DEV * HD) - mean
    variance = jnp.sum(stats[:, 1] + (HEADS_DEV * HD) * shift * shift, 0) / D
    scale = lax.rsqrt(variance + 1e-05)
    return ((joined - mean[:, None]) * scale[:, None] * out_gain).astype(bf16)


def solution(mesh):
    fine = Mesh(mesh.devices.reshape(8, 2, 4, 4, 2), ("zc", "zi", "x", "y", "core"))
    ctx, tp = ("zc", "zi", "x"), ("y", "core")
    placed = (
        P(ctx, None),
        P(ctx, None, tp),
        P(ctx, tp),
        P(tp, None, None),
        P(tp, None, None),
        P(tp, None),
        P(tp, None),
        P(tp, None),
        P(tp, None),
        P(tp),
        P(tp),
    )
    return jax.shard_map(local, mesh=fine, in_specs=placed, out_specs=P(ctx, tp), check_vma=False)
```
